256 devices in a mesh: pb: 8 (over x, core), ka: 32 (over y, z).
Axes of the slice: x: 4, y: 4, z: 8, core: 2. Of those that a mesh axis runs over, the one named last changes fastest.
Arguments:
- queries: bfloat16 [64, 32768], P(None, ('pb', 'ka')), may hold values from -6 to 6
- keys: bfloat16 [64, 32768], P(None, ('ka', 'pb')), may hold values from -6 to 6
- values: bfloat16 [64, 32768], P(None, ('ka', 'pb')), may hold values from -7.5 to 7.5
- out_grads: bfloat16 [64, 32768], P(None, ('pb', 'ka')), may hold values from -7.5 to 7.5
- row_scales: bfloat16 [3, 32768], P(None, ('pb', 'ka')), as said below
- column_scales: bfloat16 [3, 32768], P(None, ('ka', 'pb')), as said below
Outputs:
- grad_queries: float32 [64, 32768], P(None, ('pb', 'ka'))
- grad_keys: float32 [64, 32768], P(None, ('ka', 'pb'))
- grad_values: float32 [64, 32768], P(None, ('ka', 'pb'))
The draws below stay inside these ranges and needn't reach their ends.
Inputs may be any that keep to these rules, and one draw needn't show every extreme that they name: `row_scales`: positive. `column_scales`: positive.
All inputs are finite; a program needn't handle non-finite values.
Results may differ from the reference program's by a relative error of at most 0.0021.
Values may be sent and summed in bfloat16 or wider, within the bound.
A program may use at most 128 MiB of HBM per device.

```python
import jax
import jax.numpy as jnp
from jax import lax

HEAD = 64
ITERS = 3
SEQ = 32768


def draw_row_scales(key, part):
    key = jax.random.fold_in(key, 11)
    noise = jax.random.uniform(key, (ITERS, SEQ), jnp.float32, -0.8, 0.8)
    return (jnp.exp(noise) / (1.6 * SEQ)).astype(jnp.bfloat16)


def draw_column_scales(key, part):
    key = jax.random.fold_in(key, 23)
    noise = jax.random.uniform(key, (ITERS, SEQ), jnp.float32, -0.8, 0.8)
    return jnp.exp(noise).astype(jnp.bfloat16)


def feature_offset(key, lowest, highest):
    sign_key, size_key = jax.random.split(key)
    sign_column = jax.random.rademacher(sign_key, (HEAD, 1), jnp.float32)
    size_column = jax.random.uniform(size_key, (HEAD, 1), jnp.float32, lowest, highest)
    return sign_column * size_column


def draw_values(key, part):
    key = jax.random.fold_in(key, 31)
    noise_key, offset_key = jax.random.split(key)
    noise_draw = jax.random.truncated_normal(noise_key, -6.0, 6.0, (HEAD, SEQ), jnp.float32)
    offset = feature_offset(offset_key, 0.5, 1.0)
    return (noise_draw + offset).astype(jnp.bfloat16)


def draw_out_grads(key, part):
    key = jax.random.fold_in(key, 47)
    noise_key, offset_key = jax.random.split(key)
    noise_draw = jax.random.truncated_normal(noise_key, -6.0, 6.0, (HEAD, SEQ), jnp.float32)
    offset = feature_offset(offset_key, 0.5, 1.0)
    return (noise_draw + offset).astype(jnp.bfloat16)


def shard_levels(rng, dims, cuts, smallest, top_value):
    loudness, own = 1.0, jax.random.fold_in(rng, 6)
    for axis_at, parts in cuts:
        steps = jnp.exp(jax.random.uniform(jax.random.fold_in(own, axis_at), (parts,), jnp.float32, smallest / len(cuts), top_value / len(cuts)))
        loudness = loudness * jnp.repeat(steps, dims[axis_at] // parts).reshape([-1 if axis == axis_at else 1 for axis in range(len(dims))])
    return loudness


def bell_draw(key, shape, width, reach, cuts=(), held_as=jnp.bfloat16):
    entries = width * jax.random.normal(key, shape, jnp.float32)
    if cuts:
        entries = entries * shard_levels(key, shape, cuts, -0.22, 0.18)
    return jnp.clip(entries, -reach, reach).astype(held_as)


def setup_inputs(seed: int = 0) -> dict:
    key_of = jax.random.split(jax.random.key(seed), 7)
    queries = bell_draw(key_of[0], (HEAD, SEQ), 1.0, 6.0, ((1, 256),))
    keys = bell_draw(key_of[1], (HEAD, SEQ), 1.0, 6.0, ((1, 256),))
    values = draw_values(jax.random.fold_in(key_of[6], 71), 0)
    out_grads = draw_out_grads(jax.random.fold_in(key_of[6], 71), 0)
    row_scales = draw_row_scales(jax.random.fold_in(key_of[6], 71), 0)
    column_scales = draw_column_scales(jax.random.fold_in(key_of[6], 71), 0)
    return {"queries": queries, "keys": keys, "values": values, "out_grads": out_grads, "row_scales": row_scales, "column_scales": column_scales}


HIGH = lax.Precision.HIGHEST


def reference(queries, keys, values, out_grads, row_scales, column_scales):
    block = min(1024, SEQ)
    count = SEQ // block
    scale = HEAD ** -0.5
    q32 = queries.astype(jnp.float32)
    k32 = keys.astype(jnp.float32)
    v32 = values.astype(jnp.float32)
    g32 = out_grads.astype(jnp.float32)
    a = row_scales.astype(jnp.float32)
    b = column_scales.astype(jnp.float32)
    starts = (jnp.arange(count) * block).astype(jnp.int32)

    def tile(start):
        qb = lax.dynamic_slice_in_dim(q32, start, block, 1)
        return jnp.exp(jnp.dot(qb.T, k32, precision=HIGH) * scale)

    def rows_of(vec, start):
        return lax.dynamic_slice_in_dim(vec, start, block, 0)

    def first_pass(carry, start):
        kern = tile(start)
        gb = lax.dynamic_slice_in_dim(g32, start, block, 1)
        dprobs = jnp.dot(gb.T, v32, precision=HIGH)
        weighted = kern * (rows_of(a[ITERS - 1], start)[:, None] * b[ITERS - 1][None, :]) * dprobs
        return carry + jnp.sum(weighted, 0), jnp.sum(weighted, 1)

    column_total, row_total = lax.scan(first_pass, jnp.zeros((SEQ,), jnp.float32), starts)
    row_total = row_total.reshape(SEQ)

    def row_apply(vec):
        def step(carry, start):
            return carry, jnp.dot(tile(start), vec, precision=HIGH)
        return lax.scan(step, jnp.float32(0.0), starts)[1].reshape(SEQ)

    def column_apply(vec):
        def step(carry, start):
            return carry + jnp.dot(rows_of(vec, start), tile(start), precision=HIGH), None
        return lax.scan(step, jnp.zeros((SEQ,), jnp.float32), starts)[0]

    dg = [None] * (ITERS + 1)
    df = [None] * (ITERS + 1)
    dg[ITERS] = -column_total
    df[ITERS] = -row_total - a[ITERS - 1] * row_apply(b[ITERS - 1] * dg[ITERS])
    for t in range(ITERS - 1, 0, -1):
        dg[t] = -b[t - 1] * column_apply(a[t] * df[t + 1])
        df[t] = -a[t - 1] * row_apply(b[t - 1] * dg[t])
    ones = jnp.ones((SEQ,), jnp.float32)

    def last_pass(carry, start):
        grad_k, grad_v = carry
        kern = tile(start)
        qb = lax.dynamic_slice_in_dim(q32, start, block, 1)
        gb = lax.dynamic_slice_in_dim(g32, start, block, 1)
        dprobs = jnp.dot(gb.T, v32, precision=HIGH)
        a_last = rows_of(a[ITERS - 1], start)
        bracket = a_last[:, None] * (b[ITERS - 1][None, :] * (dprobs + dg[ITERS][None, :]))
        for t in range(1, ITERS + 1):
            before = ones if t == 1 else b[t - 2]
            bracket = bracket + rows_of(a[t - 1], start)[:, None] * (before[None, :] * rows_of(df[t], start)[:, None])
        for t in range(1, ITERS):
            bracket = bracket + rows_of(a[t - 1], start)[:, None] * (b[t - 1][None, :] * dg[t][None, :])
        dscores = (kern * bracket).astype(jnp.bfloat16).astype(jnp.float32)
        probs = (kern * (a_last[:, None] * b[ITERS - 1][None, :])).astype(jnp.bfloat16).astype(jnp.float32)
        grad_q = jnp.dot(k32, dscores.T, precision=HIGH) * scale
        grad_k = grad_k + jnp.dot(qb, dscores, precision=HIGH) * scale
        grad_v = grad_v + jnp.dot(gb, probs, precision=HIGH)
        return (grad_k, grad_v), grad_q

    zeros = jnp.zeros((HEAD, SEQ), jnp.float32)
    (grad_keys, grad_values), grad_blocks = lax.scan(last_pass, (zeros, zeros), starts)
    grad_queries = jnp.transpose(grad_blocks, (1, 0, 2)).reshape(HEAD, SEQ)
    return grad_queries, grad_keys, grad_values
```

```python
import functools
import math

import jax
import jax.numpy as jnp
from jax import lax
from jax.experimental import pallas as pl
from jax.experimental.pallas import tpu as pltpu
from jax.sharding import PartitionSpec as P

F32, BF16 = jnp.float32, jnp.bfloat16
MESH = pl.DeviceIdType.MESH
GROUP = 16
BLOCK = 128
HEAD = 64
LONG = GROUP * BLOCK
MSG = 2 * HEAD + 16
SCALE = HEAD ** -0.5
EXP2_SCALE = SCALE * math.log2(math.e)
JT, IT = 256, 512
LOW = 3 * HEAD


def split3(x):
    hi = x.astype(BF16).astype(F32)
    rest = x - hi
    mid = rest.astype(BF16).astype(F32)
    return hi, mid, rest - mid


def kernel(
    q_ref, k_ref, v_ref, g_ref, rs_ref, cs_ref,
    gq_ref, gk_ref, gv_ref,
    qall, kall, kern, kT, lj, fi, fif, ljf, qcat, gcat, kcat,
    a_p, b_p, vec, ub, b3b, w8, r8, cacc, ar,
    gqp, gkp, gvp, gqr, gkr, gvr,
    send_sem, recv_sem,
):
    pb, ka = lax.axis_index("pb"), lax.axis_index("ka")
    x, core, y, z = pb // 2, pb % 2, ka // 8, ka % 8
    me_a = z * 2 + core
    me_b = x * 4 + y

    def dev_a(p):
        return (x * 2 + p % 2, y * 8 + p // 2)

    def dev_b(p):
        return ((p // 4) * 2 + core, (p % 4) * 8 + z)

    barrier = pltpu.get_barrier_semaphore()

    def greet(d, _):
        pl.semaphore_signal(barrier, inc=1, device_id=dev_a((me_a + d) % GROUP), device_id_type=MESH)
        pl.semaphore_signal(barrier, inc=1, device_id=dev_b((me_b + d) % GROUP), device_id_type=MESH)
        return 0

    lax.fori_loop(1, GROUP, greet, 0)

    pad = jnp.zeros((13, BLOCK), F32)
    qall[me_a, 0:HEAD, :] = q_ref[...]
    qall[me_a, HEAD:2 * HEAD, :] = g_ref[...]
    qall[me_a, 2 * HEAD:MSG, :] = jnp.concatenate([rs_ref[...].astype(F32), pad], 0).astype(BF16)
    kall[me_b, 0:HEAD, :] = k_ref[...]
    kall[me_b, HEAD:2 * HEAD, :] = v_ref[...]
    kall[me_b, 2 * HEAD:MSG, :] = jnp.concatenate([cs_ref[...].astype(F32), pad], 0).astype(BF16)
    pl.semaphore_wait(barrier, 2 * (GROUP - 1))

    def copy(src, dst, n, device):
        return pltpu.make_async_remote_copy(
            src_ref=src, dst_ref=dst, send_sem=send_sem.at[n], recv_sem=recv_sem.at[n],
            device_id=device, device_id_type=MESH,
        )

    def broadcast(buf, me, dev, n):
        def go(d, _):
            copy(buf.at[me], buf.at[me], n, dev((me + d) % GROUP)).start()
            return 0
        lax.fori_loop(1, GROUP, go, 0)

    def scatter(buf, got, me, dev, n):
        def go(d, _):
            p = (me + d) % GROUP
            copy(buf.at[p], got.at[me], n, dev(p)).start()
            return 0
        lax.fori_loop(1, GROUP, go, 0)

    def wait_recv(buf, n):
        part = buf.at[pl.ds(0, GROUP - 1)]
        pltpu.make_async_copy(part, part, recv_sem.at[n]).wait()

    def wait_send(buf, n):
        part = buf.at[pl.ds(0, GROUP - 1)]
        pltpu.make_async_copy(part, part, send_sem.at[n]).wait()

    broadcast(kall, me_b, dev_b, 0)
    broadcast(qall, me_a, dev_a, 1)
    fif[...] = jnp.zeros_like(fif)
    ljf[...] = jnp.zeros_like(ljf)
    r8[...] = jnp.zeros_like(r8)

    wait_recv(kall, 0)

    def lanes(b):
        return pl.ds(pl.multiple_of(b * BLOCK, BLOCK), BLOCK)

    def prep_keys(b, _):
        at = lanes(b)
        kb = kall[b, 0:HEAD, :]
        kcat[:, at] = kb
        scales = kall[b, 2 * HEAD:MSG, :].astype(F32)
        for t in range(3):
            b_p[t, pl.ds(b, 1), :] = scales[t:t + 1]
        bv = kall[b, HEAD:2 * HEAD, :].astype(F32) * scales[2:3]
        hi = bv.astype(BF16).astype(F32)
        lo = bv - hi
        zero = jnp.zeros((HEAD, BLOCK), F32)
        lj[at, 0:128] = jnp.concatenate([hi, hi], 0).T.astype(BF16)
        lj[at, 128:256] = jnp.concatenate([lo, zero], 0).T.astype(BF16)
        kT[at, :] = jnp.concatenate([kb.astype(F32), zero], 0).T[:, 0:HEAD].astype(BF16)
        b3b[at, :] = jnp.broadcast_to(scales[2:3], (BLOCK, BLOCK)).T
        return 0

    lax.fori_loop(0, GROUP, prep_keys, 0)
    wait_recv(qall, 1)

    def prep_queries(b, _):
        at = lanes(b)
        qcat[:, at] = qall[b, 0:HEAD, :]
        gb = qall[b, HEAD:2 * HEAD, :]
        gcat[:, at] = gb
        scales = qall[b, 2 * HEAD:MSG, :].astype(F32)
        for t in range(3):
            a_p[t, pl.ds(b, 1), :] = scales[t:t + 1]
        ag = gb.astype(F32) * scales[2:3]
        hi = ag.astype(BF16)
        lo = (ag - hi.astype(F32)).astype(BF16)
        fi[0:64, at] = hi
        fi[64:128, at] = lo
        fi[128:192, at] = hi
        fi[192:256, at] = jnp.zeros((HEAD, BLOCK), BF16)
        return 0

    lax.fori_loop(0, GROUP, prep_queries, 0)

    def tiles(body):
        def go(n, _):
            jt, it = n // (LONG // IT), n % (LONG // IT)
            body(jt, it, pl.ds(pl.multiple_of(jt * JT, JT), JT), pl.ds(pl.multiple_of(it * IT, IT), IT))
            return 0
        return go

    def first(jt, it, js, ls):
        s = jnp.dot(kT[js, :], qcat[:, ls], preferred_element_type=F32)
        e = jnp.exp2(s * EXP2_SCALE)
        kern[js, ls] = e
        w = e * jnp.dot(lj[js, :], fi[:, ls], preferred_element_type=F32)
        r8[:, ls] += jnp.sum(w.reshape(JT // 8, 8, IT), 0)
        part = w[:, 0:128]
        for n in range(1, IT // 128):
            part = part + w[:, n * 128:(n + 1) * 128]

        @pl.when(it == 0)
        def _():
            cacc[js, :] = part

        @pl.when(it > 0)
        def _():
            cacc[js, :] += part

    lax.fori_loop(0, (LONG // JT) * (LONG // IT), tiles(first), 0)

    def column_block(b, acc, r):
        ar[r, me_b, pl.ds(b, 1), :] = jnp.sum(acc.T, 0, keepdims=True)

    def column_first(b, _):
        column_block(b, cacc[lanes(b), :], 0)
        return 0

    lax.fori_loop(0, GROUP, column_first, 0)

    def total(r):
        return jnp.sum(ar[r], 0)

    def spread_keys():
        def go(b, _):
            ub[lanes(b), :] = jnp.broadcast_to(vec[pl.ds(b, 1), :], (BLOCK, BLOCK)).T
            return 0
        lax.fori_loop(0, GROUP, go, 0)

    def spread_queries():
        for b in range(GROUP):
            w8[:, b * 128:(b + 1) * 128] = jnp.broadcast_to(vec[b:b + 1, :], (8, BLOCK))

    def column_apply(r):
        def go(b, _):
            at = lanes(b)
            acc = kern[at, 0:128] * w8[0:1, 0:128]
            for n in range(1, GROUP):
                acc = acc + kern[at, n * 128:(n + 1) * 128] * w8[0:1, n * 128:(n + 1) * 128]
            column_block(b, acc, r)
            return 0
        lax.fori_loop(0, GROUP, go, 0)

    WIDE = 8

    def row_apply(store):
        for half in range(GROUP // WIDE):
            def go(c, accs):
                js = pl.ds(pl.multiple_of(c * 64, 64), 64)
                u = ub[js, :]
                new = []
                for n in range(WIDE):
                    o = (half * WIDE + n) * 128
                    prod = kern[js, o:o + 128] * u
                    new.append(accs[n] + jnp.sum(prod.reshape(8, 8, 128), 0))
                return tuple(new)
            accs = lax.fori_loop(0, LONG // 64, go, tuple(jnp.zeros((8, BLOCK), F32) for _ in range(WIDE)))
            for n in range(WIDE):
                store(half * WIDE + n, accs[n])

    def grad_value_tiles(j0, j1):
        def body(jt, it, js, ls):
            b3 = b3b[js, :]
            a3 = fif[63:64, ls]
            probs = (kern[js, ls] * (a3 * jnp.concatenate([b3] * (IT // 128), 1))).astype(BF16)
            part = lax.dot_general(gcat[:, ls], probs, (((1,), (1,)), ((), ())), preferred_element_type=F32)
            for n in range(JT // 128):
                at = jt * (JT // 128) + n

                @pl.when(it == 0)
                def _():
                    gvp[at] = part[:, n * 128:(n + 1) * 128]

                @pl.when(it > 0)
                def _():
                    gvp[at] += part[:, n * 128:(n + 1) * 128]
        lax.fori_loop(j0 * (LONG // IT), j1 * (LONG // IT), tiles(body), 0)

    def put_rows(dst, rows, value):
        for n, piece in zip(rows, value):
            vec[...] = piece
            for b in range(GROUP):
                dst[n:n + 1, b * 128:(b + 1) * 128] = vec[b:b + 1, :]

    broadcast(ar.at[0], me_b, dev_b, 2)
    put_rows(fif, [63], [a_p[2]])
    for n, t in ((0, 2), (3, 1), (6, 0)):
        put_rows(fif, [n, n + 1, n + 2], [a_p[t]] * 3)
    for n, t in ((9, 1), (12, 0)):
        put_rows(ljf, [n, n + 1, n + 2], [b_p[t]] * 3)
    ljf[15:18, :] = jnp.ones((3, LONG), F32)
    grad_value_tiles(0, 2)

    for t in (2, 1, 0):
        r = 2 * (2 - t)
        wait_recv(ar.at[r], 2 + r)
        dg = -total(r)
        if t < 2:
            dg = b_p[t] * dg
        bdg = b_p[t] * dg
        vec[...] = bdg
        spread_keys()
        if t == 2:
            def store(n, acc):
                a = a_p[2, n:n + 1, :]
                ar[1, me_a, n:n + 1, :] = a * jnp.sum(acc, 0, keepdims=True) + jnp.sum(
                    r8[:, n * 128:(n + 1) * 128], 0, keepdims=True)
        else:
            def store(n, acc, r=r):
                ar[r + 1, me_a, n:n + 1, :] = jnp.sum(acc, 0, keepdims=True)
        row_apply(store)
        broadcast(ar.at[r + 1], me_a, dev_a, 3 + r)
        put_rows(ljf, [3 * (2 - t) + n for n in range(3)], split3(bdg))
        if t == 2:
            grad_value_tiles(2, 5)
        elif t == 1:
            scatter(gvp, gvr, me_b, dev_b, 8)
        else:
            def late_keys(b, _):
                at = lanes(b)
                zero = jnp.zeros((HEAD, BLOCK), F32)
                low = jnp.concatenate([ljf[:, at], zero], 0).T[:, 0:HEAD]
                lj[at, LOW:LOW + HEAD] = low.astype(BF16)
                return 0
            lax.fori_loop(0, GROUP, late_keys, 0)
        wait_recv(ar.at[r + 1], 3 + r)
        df = -total(r + 1)
        if t < 2:
            df = a_p[t] * df
        adf = a_p[t] * df
        if t > 0:
            vec[...] = adf
            spread_queries()
            column_apply(r + 2)
            broadcast(ar.at[r + 2], me_b, dev_b, 4 + r)
            if t == 2:
                grad_value_tiles(5, 8)
        put_rows(fif, [9 + 3 * (2 - t) + n for n in range(3)], split3(adf))

    fi[LOW:LOW + HEAD, :] = fif[...].astype(BF16)
    gqp[...] = jnp.zeros_like(gqp)

    def last(jt, it, js, ls):
        bracket = jnp.dot(lj[js, :], fi[:, ls], preferred_element_type=F32)
        ds = (kern[js, ls] * bracket).astype(BF16)
        part = jnp.dot(kcat[:, js], ds, preferred_element_type=F32)
        for n in range(IT // 128):
            gqp[it * (IT // 128) + n] += part[:, n * 128:(n + 1) * 128]
        part = lax.dot_general(qcat[:, ls], ds, (((1,), (1,)), ((), ())), preferred_element_type=F32)
        for n in range(JT // 128):
            at = jt * (JT // 128) + n

            @pl.when(it == 0)
            def _():
                gkp[at] = part[:, n * 128:(n + 1) * 128]

            @pl.when(it > 0)
            def _():
                gkp[at] += part[:, n * 128:(n + 1) * 128]

    lax.fori_loop(0, (LONG // JT) * (LONG // IT), tiles(last), 0)

    scatter(gqp, gqr, me_a, dev_a, 9)
    scatter(gkp, gkr, me_b, dev_b, 10)
    gvr[me_b] = gvp[me_b]
    gqr[me_a] = gqp[me_a]
    gkr[me_b] = gkp[me_b]
    wait_recv(gvr, 8)
    gv_ref[...] = jnp.sum(gvr[...], 0)
    wait_recv(gqr, 9)
    gq_ref[...] = jnp.sum(gqr[...], 0) * SCALE
    wait_recv(gkr, 10)
    gk_ref[...] = jnp.sum(gkr[...], 0) * SCALE
    wait_send(kall, 0)
    wait_send(qall, 1)
    for r in range(6):
        wait_send(ar.at[r], 2 + r)
    wait_send(gvp, 8)
    wait_send(gqp, 9)
    wait_send(gkp, 10)


def body(queries, keys, values, out_grads, row_scales, column_scales):
    out = jax.ShapeDtypeStruct((HEAD, BLOCK), F32)
    vmem = pl.BlockSpec(memory_space=pltpu.VMEM)
    part = pltpu.VMEM((GROUP, HEAD, BLOCK), F32)
    return pl.pallas_call(
        kernel,
        out_shape=(out, out, out),
        in_specs=[vmem] * 6,
        out_specs=(vmem,) * 3,
        scratch_shapes=[
            pltpu.VMEM((GROUP, MSG, BLOCK), BF16),
            pltpu.VMEM((GROUP, MSG, BLOCK), BF16),
            pltpu.VMEM((LONG, LONG), F32),
            pltpu.VMEM((LONG, HEAD), BF16),
            pltpu.VMEM((LONG, 4 * HEAD), BF16),
            pltpu.VMEM((4 * HEAD, LONG), BF16),
            pltpu.VMEM((HEAD, LONG), F32),
            pltpu.VMEM((HEAD, LONG), F32),
            pltpu.VMEM((HEAD, LONG), BF16),
            pltpu.VMEM((HEAD, LONG), BF16),
            pltpu.VMEM((HEAD, LONG), BF16),
            pltpu.VMEM((3, GROUP, BLOCK), F32),
            pltpu.VMEM((3, GROUP, BLOCK), F32),
            pltpu.VMEM((GROUP, BLOCK), F32),
            pltpu.VMEM((LONG, BLOCK), F32),
            pltpu.VMEM((LONG, BLOCK), F32),
            pltpu.VMEM((8, LONG), F32),
            pltpu.VMEM((8, LONG), F32),
            pltpu.VMEM((LONG, BLOCK), F32),
            pltpu.VMEM((6, GROUP, GROUP, BLOCK), F32),
            part, part, part, part, part, part,
            pltpu.SemaphoreType.DMA((11,)),
            pltpu.SemaphoreType.DMA((11,)),
        ],
        compiler_params=pltpu.CompilerParams(
            collective_id=0, has_side_effects=True, vmem_limit_bytes=56 * 2**20),
    )(queries, keys, values, out_grads, row_scales, column_scales)


def solution(mesh):
    in_specs = (
        P(None, ("pb", "ka")),
        P(None, ("ka", "pb")),
        P(None, ("ka", "pb")),
        P(None, ("pb", "ka")),
        P(None, ("pb", "ka")),
        P(None, ("ka", "pb")),
    )
    out_specs = (P(None, ("pb", "ka")), P(None, ("ka", "pb")), P(None, ("ka", "pb")))
    return jax.shard_map(body, mesh=mesh, in_specs=in_specs, out_specs=out_specs, check_vma=False)
```

```python
import math

import jax
import jax.numpy as jnp
from jax import lax
from jax.experimental import pallas as pl
from jax.experimental.pallas import tpu as pltpu
from jax.sharding import PartitionSpec as P

F32, BF16 = jnp.float32, jnp.bfloat16
MESH = pl.DeviceIdType.MESH
GROUP = 16
HALF = 8
BLOCK = 128
HEAD = 64
LONG = GROUP * BLOCK
WIDE = HALF * BLOCK
MSG = HEAD + 16
SCALE = HEAD ** -0.5
EXP2_SCALE = SCALE * math.log2(math.e)
LOW = 3 * HEAD
FAR_Z = (4, 3, 5, 2, 6, 1, 7)
FAR_ZC = tuple((dz, dc) for dz in FAR_Z for dc in (0, 1)) + ((0, 1),)
FAR_XY = ((2, 2), (1, 2), (2, 1), (3, 2), (2, 3), (1, 1), (3, 3), (1, 3), (3, 1),
          (0, 2), (2, 0), (0, 1), (1, 0), (0, 3), (3, 0))
K_IN, V_IN, Q_IN, G_IN, Q_SIB, G_SIB, AR, GV, GQ_SIB, GQ, GK = 0, 1, 2, 3, 4, 5, 6, 12, 13, 14, 15
N_SEM = 16


def split3(x):
    hi = x.astype(BF16).astype(F32)
    rest = x - hi
    mid = rest.astype(BF16).astype(F32)
    return hi, mid, rest - mid


def kernel(
    q_ref, k_ref, v_ref, g_ref, rs_ref, cs_ref,
    out_ref,
    qs, gs, ks, vs, kern, kT, qT, gT, lj, fi, fif, ljf, qcat, kcat,
    a_p, b_p, vec, ub, b3b, w8, r8, cacc, ar,
    gvt, gkt, gqp, gkp, gvp, gqs, gqr, gkr, gvr,
    send_sem, recv_sem,
):
    pb, ka = lax.axis_index("pb"), lax.axis_index("ka")
    x, core, y, z = pb // 2, pb % 2, ka // 8, ka % 8
    me_a = core * HALF + z
    me_b = x * 4 + y
    sibling = (x * 2 + 1 - core, ka)

    def dev_z(dz, dc):
        return (x * 2 + (core + dc) % 2, y * 8 + (z + dz) % 8)

    def dev_xy(dx, dy):
        return (((x + dx) % 4) * 2 + core, ((y + dy) % 4) * 8 + z)

    barrier = pltpu.get_barrier_semaphore()
    for d in FAR_XY:
        pl.semaphore_signal(barrier, inc=1, device_id=dev_xy(*d), device_id_type=MESH)
    for d in FAR_ZC:
        pl.semaphore_signal(barrier, inc=1, device_id=dev_z(*d), device_id_type=MESH)

    pad = jnp.zeros((13, BLOCK), F32)
    ks[me_b] = k_ref[...]
    qs[me_a] = q_ref[...]
    vs[me_b, 0:HEAD, :] = v_ref[...]
    vs[me_b, HEAD:MSG, :] = jnp.concatenate([cs_ref[...].astype(F32), pad], 0).astype(BF16)
    gs[me_a, 0:HEAD, :] = g_ref[...]
    gs[me_a, HEAD:MSG, :] = jnp.concatenate([rs_ref[...].astype(F32), pad], 0).astype(BF16)
    pl.semaphore_wait(barrier, 2 * (GROUP - 1))

    def send(src, dst, n, device):
        pltpu.make_async_remote_copy(
            src_ref=src, dst_ref=dst, send_sem=send_sem.at[n], recv_sem=recv_sem.at[n],
            device_id=device, device_id_type=MESH,
        ).start()

    def to_xy(buf, n):
        for d in FAR_XY:
            send(buf.at[me_b], buf.at[me_b], n, dev_xy(*d))

    def to_zc(buf, n):
        for d in FAR_ZC:
            send(buf.at[me_a], buf.at[me_a], n, dev_z(*d))

    def to_z(buf, n):
        for dz in FAR_Z:
            send(buf.at[me_a], buf.at[me_a], n, dev_z(dz, 0))

    def own_half(buf):
        return buf.at[pl.ds(pl.multiple_of(core * HALF, HALF), HALF)]

    def wait(sem, n, part):
        pltpu.make_async_copy(part, part, sem.at[n]).wait()

    def wait_recv(buf, n, count):
        wait(recv_sem, n, buf.at[pl.ds(0, count)])

    def wait_send(buf, n, count):
        wait(send_sem, n, buf.at[pl.ds(0, count)])

    to_xy(ks, K_IN)
    to_z(qs, Q_IN)
    to_xy(vs, V_IN)
    to_z(gs, G_IN)

    fif[...] = jnp.zeros_like(fif)
    ljf[...] = jnp.zeros_like(ljf)
    r8[...] = jnp.zeros_like(r8)
    fi[LOW:LOW + HEAD, :] = jnp.zeros((HEAD, LONG), BF16)
    zero = jnp.zeros((HEAD, BLOCK), F32)

    def turned(block):
        return jnp.concatenate([block.astype(F32), zero], 0).T[:, 0:HEAD]

    def lanes(b):
        return pl.ds(pl.multiple_of(b * BLOCK, BLOCK), BLOCK)

    wait_recv(ks, K_IN, GROUP - 1)
    for b in range(GROUP):
        kcat[:, b * BLOCK:(b + 1) * BLOCK] = ks[b]
        kT[b * BLOCK:(b + 1) * BLOCK, :] = turned(ks[b]).astype(BF16)

    def prep_q(h):
        for n in range(HALF):
            b = h * HALF + n
            qcat[:, lanes(b)] = qs[b]

    def prep_g(h):
        for n in range(HALF):
            b = h * HALF + n
            gb = gs[b, 0:HEAD, :]
            scales = gs[b, HEAD:MSG, :].astype(F32)
            for t in range(3):
                a_p[t, pl.ds(b, 1), :] = scales[t:t + 1]
            ag = gb.astype(F32) * scales[2:3]
            hi = ag.astype(BF16)
            at = lanes(b)
            fi[0:64, at] = hi
            fi[64:128, at] = (ag - hi.astype(F32)).astype(BF16)
            fi[128:192, at] = hi

    TALL = 512

    def half_tiles(h, body):
        ls = pl.ds(pl.multiple_of(h * WIDE, WIDE), WIDE)

        def go(n, _):
            body(pl.ds(pl.multiple_of(n * TALL, TALL), TALL), ls)
            return 0
        lax.fori_loop(0, LONG // TALL, go, 0)

    def score_tile(js, ls):
        s = jnp.dot(kT[js, :], qcat[:, ls], preferred_element_type=F32)
        kern[js, ls] = jnp.exp2(s * EXP2_SCALE)

    def weigh(fresh):
        def body(js, ls):
            w = kern[js, ls] * jnp.dot(lj[js, :], fi[:, ls], preferred_element_type=F32)
            r8[:, ls] += jnp.sum(w.reshape(TALL // 8, 8, WIDE), 0)
            part = w[:, 0:128]
            for n in range(1, HALF):
                part = part + w[:, n * 128:(n + 1) * 128]
            if fresh:
                cacc[js, :] = part
            else:
                cacc[js, :] += part
        return body

    wait_recv(qs, Q_IN, HALF - 1)
    send(own_half(qs), own_half(qs), Q_SIB, sibling)
    prep_q(core)
    half_tiles(core, score_tile)
    wait_recv(gs, G_IN, HALF - 1)
    send(own_half(gs), own_half(gs), G_SIB, sibling)
    wait_recv(qs, Q_SIB, HALF)
    prep_q(1 - core)
    half_tiles(1 - core, score_tile)

    wait_recv(vs, V_IN, GROUP - 1)
    for b in range(GROUP):
        rows = slice(b * BLOCK, (b + 1) * BLOCK)
        scales = vs[b, HEAD:MSG, :].astype(F32)
        for t in range(3):
            b_p[t, b:b + 1, :] = scales[t:t + 1]
        bv = vs[b, 0:HEAD, :].astype(F32) * scales[2:3]
        hi = bv.astype(BF16).astype(F32)
        lj[rows, 0:128] = jnp.concatenate([hi, hi], 0).T.astype(BF16)
        lj[rows, 128:256] = jnp.concatenate([bv - hi, zero], 0).T.astype(BF16)
    prep_g(core)
    half_tiles(core, weigh(True))
    wait_recv(gs, G_SIB, HALF)
    prep_g(1 - core)
    half_tiles(1 - core, weigh(False))

    def column_block(b, acc, r):
        ar[r, me_b, b:b + 1, :] = jnp.sum(acc.T, 0, keepdims=True)

    for b in range(GROUP):
        column_block(b, cacc[b * BLOCK:(b + 1) * BLOCK, :], 0)

    def total(r):
        return jnp.sum(ar[r], 0)

    def spread_keys(dst, src):
        for b in range(GROUP):
            dst[b * BLOCK:(b + 1) * BLOCK, :] = jnp.broadcast_to(src[b:b + 1, :], (BLOCK, BLOCK)).T

    def spread_queries():
        for b in range(GROUP):
            w8[:, b * 128:(b + 1) * 128] = jnp.broadcast_to(vec[b:b + 1, :], (8, BLOCK))

    def column_apply(r):
        for b in range(GROUP):
            at = slice(b * BLOCK, (b + 1) * BLOCK)
            acc = kern[at, 0:128] * w8[0:1, 0:128]
            for n in range(1, GROUP):
                acc = acc + kern[at, n * 128:(n + 1) * 128] * w8[0:1, n * 128:(n + 1) * 128]
            column_block(b, acc, r)

    def row_apply(store):
        def go(c, accs):
            js = pl.ds(pl.multiple_of(c * 64, 64), 64)
            u = ub[js, :]
            return tuple(
                accs[n] + jnp.sum((kern[js, n * 128:(n + 1) * 128] * u).reshape(8, 8, 128), 0)
                for n in range(GROUP))
        accs = lax.fori_loop(
            0, LONG // 64, go, tuple(jnp.zeros((8, BLOCK), F32) for _ in range(GROUP)), unroll=2)
        for n in range(GROUP):
            store(n, accs[n])

    def value_tile(n, _):
        js = pl.ds(pl.multiple_of(n * TALL, TALL), TALL)
        b3 = b3b[js, :]
        scale = fif[63:64, :] * jnp.concatenate([b3] * GROUP, 1)
        probs = (kern[js, :] * scale).astype(BF16)
        gvt[js, :] = jnp.dot(probs, gT[...], preferred_element_type=F32)
        return 0

    def put_rows(dst, rows, value):
        for n, piece in zip(rows, value):
            vec[...] = piece
            for b in range(GROUP):
                dst[n:n + 1, b * 128:(b + 1) * 128] = vec[b:b + 1, :]

    def turn_back(block):
        wide = jnp.concatenate([block, jnp.zeros((BLOCK, BLOCK - HEAD), F32)], 1)
        return wide.T[0:HEAD, :]

    to_xy(ar.at[0], AR)
    put_rows(fif, [63], [a_p[2]])
    spread_keys(b3b, b_p.at[2])
    for b in range(GROUP):
        gT[b * BLOCK:(b + 1) * BLOCK, :] = turned(gs[b, 0:HEAD, :]).astype(BF16)
    lax.fori_loop(0, LONG // TALL, value_tile, 0)

    for t in (2, 1, 0):
        r = 2 * (2 - t)
        wait_recv(ar.at[r], AR + r, GROUP - 1)
        dg = -total(r)
        if t < 2:
            dg = b_p[t] * dg
        bdg = b_p[t] * dg
        vec[...] = bdg
        spread_keys(ub, vec)
        if t == 2:
            def store(n, acc):
                a = a_p[2, n:n + 1, :]
                ar[1, me_a, n:n + 1, :] = a * jnp.sum(acc, 0, keepdims=True) + jnp.sum(
                    r8[:, n * 128:(n + 1) * 128], 0, keepdims=True)
        else:
            def store(n, acc, r=r):
                ar[r + 1, me_a, n:n + 1, :] = jnp.sum(acc, 0, keepdims=True)
        row_apply(store)
        to_zc(ar.at[r + 1], AR + r + 1)
        put_rows(ljf, [3 * (2 - t) + n for n in range(3)], split3(bdg))
        if t == 2:
            for b in range(GROUP):
                gvp[b] = turn_back(gvt[b * BLOCK:(b + 1) * BLOCK, :])
            for dx, dy in FAR_XY:
                send(gvp.at[((x + dx) % 4) * 4 + (y + dy) % 4], gvr.at[me_b], GV, dev_xy(dx, dy))
            gvr[me_b] = gvp[me_b]
        elif t == 1:
            for b in range(GROUP):
                qT[b * BLOCK:(b + 1) * BLOCK, :] = turned(qs[b]).astype(BF16)
            for n, s in ((0, 2), (3, 1), (6, 0)):
                put_rows(fif, [n, n + 1, n + 2], [a_p[s]] * 3)
            for n, s in ((9, 1), (12, 0)):
                put_rows(ljf, [n, n + 1, n + 2], [b_p[s]] * 3)
            ljf[15:18, :] = jnp.ones((3, LONG), F32)
        else:
            for b in range(GROUP):
                rows = slice(b * BLOCK, (b + 1) * BLOCK)
                lj[rows, LOW:LOW + HEAD] = turned(ljf[:, rows]).astype(BF16)
            wait_recv(gvr, GV, GROUP - 1)
            out_ref[2] = jnp.sum(gvr[...], 0)
        wait_recv(ar.at[r + 1], AR + r + 1, GROUP - 1)
        df = -total(r + 1)
        if t < 2:
            df = a_p[t] * df
        adf = a_p[t] * df
        if t > 0:
            vec[...] = adf
            spread_queries()
            column_apply(r + 2)
            to_xy(ar.at[r + 2], AR + r + 2)
        put_rows(fif, [9 + 3 * (2 - t) + n for n in range(3)], split3(adf))

    fi[LOW:LOW + HEAD, :] = fif[...].astype(BF16)

    def last_tile(h, jt, fresh):
        ls = pl.ds(pl.multiple_of(h * WIDE, WIDE), WIDE)
        js = pl.ds(pl.multiple_of(jt * WIDE, WIDE), WIDE)
        bracket = jnp.dot(lj[js, :], fi[:, ls], preferred_element_type=F32)
        ds = (kern[js, ls] * bracket).astype(BF16)
        part = jnp.dot(kcat[:, js], ds, preferred_element_type=F32)
        turn = jnp.dot(ds, qT[ls, :], preferred_element_type=F32)

        @pl.when(jt == 0)
        def _():
            for n in range(HALF):
                gqp[h * HALF + n] = part[:, n * 128:(n + 1) * 128]

        @pl.when(jt > 0)
        def _():
            for n in range(HALF):
                gqp[h * HALF + n] += part[:, n * 128:(n + 1) * 128]
        if fresh:
            gkt[js, :] = turn
            return
        gkt[js, :] += turn
        for n in range(HALF):
            gkp[jt * HALF + n] = turn_back(gkt[lanes(jt * HALF + n), :])

    def send_keys(jt):
        for n in range(HALF):
            p = jt * HALF + n

            @pl.when(p != me_b)
            def _():
                send(gkp.at[p], gkr.at[me_b], GK, ((p // 4) * 2 + core, (p % 4) * 8 + z))

    def last_first(jt, _):
        last_tile(1 - core, jt, True)
        return 0

    lax.fori_loop(0, 2, last_first, 0)
    send(gqp.at[pl.ds(pl.multiple_of((1 - core) * HALF, HALF), HALF)], gqs, GQ_SIB, sibling)

    def last_second(jt, _):
        last_tile(core, jt, False)

        @pl.when(jt == 0)
        def _():
            send_keys(0)
        return 0

    lax.fori_loop(0, 2, last_second, 0)
    wait_recv(gqs, GQ_SIB, HALF)
    for n in range(HALF):
        gqp[core * HALF + n] += gqs[n]
    for dz in FAR_Z:
        to = (z + dz) % 8
        send(gqp.at[core * HALF + to], gqr.at[z], GQ, dev_z(dz, 0))
    send_keys(1)
    gqr[z] = gqp[me_a]
    gkr[me_b] = gkp[me_b]
    wait_recv(gqr, GQ, HALF - 1)
    out_ref[0] = jnp.sum(gqr[...], 0) * SCALE
    wait_recv(gkr, GK, GROUP - 1)
    out_ref[1] = jnp.sum(gkr[...], 0) * SCALE
    wait_send(ks, K_IN, GROUP - 1)
    wait_send(vs, V_IN, GROUP - 1)
    wait_send(qs, Q_IN, HALF - 1)
    wait_send(gs, G_IN, HALF - 1)
    wait_send(qs, Q_SIB, HALF)
    wait_send(gs, G_SIB, HALF)
    for r in range(6):
        wait_send(ar.at[r], AR + r, GROUP - 1)
    wait_send(gvp, GV, GROUP - 1)
    wait_send(gqs, GQ_SIB, HALF)
    wait_send(gqr, GQ, HALF - 1)
    wait_send(gkp, GK, GROUP - 1)


def body(queries, keys, values, out_grads, row_scales, column_scales):
    vmem = pl.BlockSpec(memory_space=pltpu.VMEM)
    parts = [pltpu.VMEM((GROUP, HEAD, BLOCK), F32)] * 3
    half = pltpu.VMEM((HALF, HEAD, BLOCK), F32)
    out = pl.pallas_call(
        kernel,
        out_shape=jax.ShapeDtypeStruct((3, HEAD, BLOCK), F32),
        in_specs=[vmem] * 6,
        out_specs=vmem,
        scratch_shapes=[
            pltpu.VMEM((GROUP, HEAD, BLOCK), BF16),
            pltpu.VMEM((GROUP, MSG, BLOCK), BF16),
            pltpu.VMEM((GROUP, HEAD, BLOCK), BF16),
            pltpu.VMEM((GROUP, MSG, BLOCK), BF16),
            pltpu.VMEM((LONG, LONG), F32),
            pltpu.VMEM((LONG, HEAD), BF16),
            pltpu.VMEM((LONG, HEAD), BF16),
            pltpu.VMEM((LONG, HEAD), BF16),
            pltpu.VMEM((LONG, 4 * HEAD), BF16),
            pltpu.VMEM((4 * HEAD, LONG), BF16),
            pltpu.VMEM((HEAD, LONG), F32),
            pltpu.VMEM((HEAD, LONG), F32),
            pltpu.VMEM((HEAD, LONG), BF16),
            pltpu.VMEM((HEAD, LONG), BF16),
            pltpu.VMEM((3, GROUP, BLOCK), F32),
            pltpu.VMEM((3, GROUP, BLOCK), F32),
            pltpu.VMEM((GROUP, BLOCK), F32),
            pltpu.VMEM((LONG, BLOCK), F32),
            pltpu.VMEM((LONG, BLOCK), F32),
            pltpu.VMEM((8, LONG), F32),
            pltpu.VMEM((8, LONG), F32),
            pltpu.VMEM((LONG, BLOCK), F32),
            pltpu.VMEM((6, GROUP, GROUP, BLOCK), F32),
            pltpu.VMEM((LONG, HEAD), F32),
            pltpu.VMEM((LONG, HEAD), F32),
            *parts, half, half, *parts[:2],
            pltpu.SemaphoreType.DMA((N_SEM,)),
            pltpu.SemaphoreType.DMA((N_SEM,)),
        ],
        compiler_params=pltpu.CompilerParams(
            collective_id=0, has_side_effects=True, vmem_limit_bytes=58 * 2**20),
    )(queries, keys, values, out_grads, row_scales, column_scales)
    return out[0], out[1], out[2]


def solution(mesh):
    in_specs = (
        P(None, ("pb", "ka")),
        P(None, ("ka", "pb")),
        P(None, ("ka", "pb")),
        P(None, ("pb", "ka")),
        P(None, ("pb", "ka")),
        P(None, ("ka", "pb")),
    )
    out_specs = (P(None, ("pb", "ka")), P(None, ("ka", "pb")), P(None, ("ka", "pb")))
    return jax.shard_map(body, mesh=mesh, in_specs=in_specs, out_specs=out_specs, check_vma=False)
```
